32 devices in a mesh: fsdp: 16 (over z, y, x), tensor: 2 (over core).
Axes of the slice: x: 2, y: 2, z: 4, core: 2. Of those that a mesh axis runs over, the one named last changes fastest.
Arguments:
- attention_output: bfloat16 [8192, 8192], P('fsdp', 'tensor'), may hold values from -6 to 6
- frozen_weight: bfloat16 [8192, 4096], P('tensor', 'fsdp'), may hold values from -0.397747564 to 0.397747564
- adapter_down: bfloat16 [8192, 64], P('tensor'), may hold values from -0.06629126 to 0.06629126
- adapter_up: bfloat16 [64, 4096], replicated, may hold values from -0.25 to 0.25
- magnitude: float32 [4096], replicated, may hold values from 0.25 to 1
- cotangent: bfloat16 [8192, 4096], P('fsdp', 'tensor'), may hold values from -3 to 3
Outputs:
- layer_out: bfloat16 [8192, 4096], P('fsdp', 'tensor')
- input_gradient: bfloat16 [8192, 8192], P('fsdp', 'tensor')
- down_gradient: float32 [8192, 64], P('tensor')
- d_up: float32 [64, 4096], P(None, 'tensor')
- d_magnitude: float32 [4096], P('tensor')
The draws below stay inside these ranges and needn't reach their ends.
All inputs are finite; a program needn't handle non-finite values.
Results may differ from the reference program's by a relative error of at most 0.0085.
Values may be sent and summed in bfloat16 or wider, within the bound.
No kernel may reach another device: no remote copies, remote signals or barrier semaphores. Data moves between devices by JAX's collectives and lax.ppermute only.
A program may use at most 192 MiB of HBM per device.

```python
import math
import jax
import jax.numpy as jnp
from jax import lax

INPUT_FEATURES = 8192
OUTPUT_FEATURES = 4096
ADAPTER_RANK = 64
TOKENS = 8192
N_TENSOR = 2


def draw_frozen_weight(key, part):
    key = jax.random.fold_in(key, 11)
    subkeys = jax.random.split(key, 3)
    entries = jax.random.truncated_normal(subkeys[0], -4.0, 4.0, (INPUT_FEATURES, OUTPUT_FEATURES), jnp.float32)
    row_scale = jnp.exp(jax.random.uniform(subkeys[1], (INPUT_FEATURES, 1), jnp.float32, math.log(0.3), math.log(3.0)))
    col_scale = jnp.exp(jax.random.uniform(subkeys[2], (1, OUTPUT_FEATURES), jnp.float32, math.log(0.3), math.log(3.0)))
    return (entries * row_scale * col_scale / math.sqrt(INPUT_FEATURES)).astype(jnp.bfloat16)


def draw_adapter_down(key, part):
    key = jax.random.fold_in(key, 23)
    subkeys = jax.random.split(key, 3)
    shared = jax.random.truncated_normal(subkeys[0], -4.0, 4.0, (INPUT_FEATURES, 1), jnp.float32)
    own = jax.random.truncated_normal(subkeys[1], -4.0, 4.0, (INPUT_FEATURES, ADAPTER_RANK), jnp.float32)
    share_weight = jax.random.uniform(subkeys[2], (1, ADAPTER_RANK), jnp.float32, 0.45, 0.8)
    own_weight = jnp.sqrt(1.0 - share_weight * share_weight)
    return ((share_weight * shared + own_weight * own) / math.sqrt(INPUT_FEATURES)).astype(jnp.bfloat16)


def shard_levels(own_key, extent, pieces, smallest, top_value):
    def one(dim, shards_of):
        heights = jax.random.uniform(jax.random.fold_in(jax.random.fold_in(own_key, 6), dim), (shards_of,), jnp.float32, smallest / len(pieces), top_value / len(pieces))
        return jnp.repeat(jnp.exp(heights), extent[dim] // shards_of).reshape((-1,) + (1,) * (len(extent) - dim - 1))

    gain = one(*pieces[0])
    for cut in pieces[1:]:
        gain = gain * one(*cut)
    return gain


def normal_values(rng, shape, width, reach, cuts=(), kind=jnp.bfloat16):
    gain = shard_levels(rng, shape, cuts, -0.22, 0.18) if cuts else 1.0
    result = jax.random.normal(rng, shape, jnp.float32) * width * gain
    return jnp.minimum(jnp.maximum(result, -reach), reach).astype(kind)


def setup_inputs(seed: int = 0) -> dict:
    keys = jax.random.split(jax.random.key(seed), 7)
    attention_output = normal_values(keys[0], (TOKENS, INPUT_FEATURES), 1.0, 6.0, ((0, 16), (1, 2)))
    frozen_weight = draw_frozen_weight(jax.random.fold_in(keys[6], 71), 0)
    adapter_down = draw_adapter_down(jax.random.fold_in(keys[6], 71), 0)
    adapter_up = normal_values(keys[3], (ADAPTER_RANK, OUTPUT_FEATURES), (OUTPUT_FEATURES // 8) ** -0.5, 0.25)
    magnitude = jnp.clip(jnp.exp(jax.random.uniform(keys[4], (OUTPUT_FEATURES,), jnp.float32, math.log(0.25), math.log(1.0))), 0.25, 1.0)
    cotangent = normal_values(keys[5], (TOKENS, OUTPUT_FEATURES), 0.5, 3.0, ((0, 16), (1, 2)))
    return {"attention_output": attention_output, "frozen_weight": frozen_weight, "adapter_down": adapter_down, "adapter_up": adapter_up, "magnitude": magnitude, "cotangent": cotangent}


eps_norm = 1e-06

def reference(attention_output, frozen_weight, adapter_down, adapter_up, magnitude, cotangent):
    block_rows = INPUT_FEATURES // N_TENSOR
    adapter_hidden = jnp.dot(attention_output, adapter_down, preferred_element_type=jnp.float32).astype(jnp.bfloat16)
    merged_weight = frozen_weight.astype(jnp.float32) + jnp.dot(adapter_down, adapter_up, preferred_element_type=jnp.float32)
    col_norms = jnp.sqrt(lax.optimization_barrier(jnp.sum(merged_weight * merged_weight, axis=0)) + eps_norm)
    frozen_output_sum = jnp.zeros((TOKENS, OUTPUT_FEATURES), jnp.float32)
    for block_index in range(N_TENSOR):
        lower = block_index * block_rows
        partial_value = jnp.dot(attention_output[:, lower:lower + block_rows], frozen_weight[lower:lower + block_rows, :], preferred_element_type=jnp.float32).astype(jnp.bfloat16)
        partial_value = lax.optimization_barrier(partial_value)
        frozen_output_sum = frozen_output_sum + partial_value.astype(jnp.float32)
    unscaled_output = frozen_output_sum + jnp.dot(adapter_hidden, adapter_up, preferred_element_type=jnp.float32)
    col_scale = magnitude / col_norms
    layer_out = (unscaled_output * col_scale[None, :]).astype(jnp.bfloat16)
    cot_float = cotangent.astype(jnp.float32)
    prescale_gradient = (cot_float * col_scale[None, :]).astype(jnp.bfloat16)
    weighted = lax.optimization_barrier(jnp.sum(cot_float * unscaled_output, axis=0)) / col_norms
    column_coefficient = -weighted * magnitude / (col_norms * col_norms)
    lowrank_gradient = jnp.dot(prescale_gradient, adapter_up.T, preferred_element_type=jnp.float32).astype(jnp.bfloat16)
    input_gradient = (jnp.dot(prescale_gradient, frozen_weight.T, preferred_element_type=jnp.float32) + jnp.dot(lowrank_gradient, adapter_down.T, preferred_element_type=jnp.float32)).astype(jnp.bfloat16)
    scaled_up_factor = (column_coefficient[:, None] * adapter_up.T.astype(jnp.float32)).astype(jnp.bfloat16)
    up_inner_product = jnp.dot(adapter_up, scaled_up_factor, preferred_element_type=jnp.float32)
    down_gradient = jnp.dot(attention_output.T, lowrank_gradient, preferred_element_type=jnp.float32) + jnp.dot(frozen_weight, scaled_up_factor, preferred_element_type=jnp.float32) + jnp.dot(adapter_down.astype(jnp.float32), up_inner_product, precision=lax.Precision.HIGHEST)
    down_gram_matrix = jnp.dot(adapter_down.T, adapter_down, preferred_element_type=jnp.float32)
    apply_projection = jnp.dot(adapter_down.T, frozen_weight, preferred_element_type=jnp.float32) + jnp.dot(down_gram_matrix, adapter_up.astype(jnp.float32), precision=lax.Precision.HIGHEST)
    d_up = jnp.dot(adapter_hidden.T, prescale_gradient, preferred_element_type=jnp.float32) + apply_projection * column_coefficient[None, :]
    grad_scale = TOKENS ** (-0.5)
    return (layer_out, input_gradient, down_gradient * grad_scale, d_up * grad_scale, weighted * grad_scale)
```

```python
import jax
import jax.numpy as jnp
from jax import lax
from jax.sharding import PartitionSpec as P

eps_norm = 1e-06
routes = ("xzy", "yzx", "zxy", "zyx")


def flip(value, axis, bit):
    pairs = [(i, i ^ bit) for i in range(lax.axis_size(axis))]
    return lax.ppermute(value, axis, pairs)


def sum_over(value, axis):
    bit = 1
    while bit < lax.axis_size(axis):
        value = value + flip(value, axis, bit)
        bit *= 2
    return value


def arrivals(z, depth):
    found = [("own", 0)]
    for hops in range(1, depth):
        if z - hops >= 0:
            found.append(("up", hops))
        if z + hops < depth:
            found.append(("down", hops))
    return found


def source_plane(z, depth):
    return [z - hops if way == "up" else z + hops for way, hops in arrivals(z, depth)]


def along_z(block, z, depth):
    count = 4 * depth
    held = {("own", 0): block}
    up = down = block
    for hops in range(1, depth):
        up = lax.ppermute(up, "fsdp", [(i, i + 4) for i in range(count - 4) if i // 4 >= hops - 1])
        down = lax.ppermute(
            down, "fsdp", [(i, i - 4) for i in range(4, count) if i // 4 + hops - 1 < depth]
        )
        held["up", hops] = up
        held["down", hops] = down
    placed = []
    for position in range(depth):
        wanted = [arrivals(plane, depth)[position] for plane in range(depth)]
        chosen = held[wanted[0]]
        for source in sorted(set(wanted) - {wanted[0]}):
            here = sum((z == plane) for plane in range(depth) if wanted[plane] == source) > 0
            chosen = jnp.where(here, held[source], chosen)
        placed.append(chosen)
    return placed


def both(block, place, bit, axis):
    other = flip(block, "fsdp", bit)
    low = jnp.where(place == 0, block, other)
    high = jnp.where(place == 0, other, block)
    return jnp.stack([low, high], axis=axis)


def gather_planes(piece, route, x, y, z, depth):
    def in_plane(block, way):
        if way == "x":
            return both(block, x, 1, block.ndim - 2)
        return both(block, y, 2, 0)

    blocks = [piece]
    for way in route:
        if way == "z":
            blocks = along_z(blocks[0], z, depth)
        else:
            blocks = [in_plane(block, way) for block in blocks]
    return [block.reshape(-1, piece.shape[-1]) for block in blocks]


def nt(a, b):
    return lax.dot_general(a, b, (((1,), (1,)), ((), ())), preferred_element_type=jnp.float32)


def nn(a, b):
    return jnp.dot(a, b, preferred_element_type=jnp.float32)


def tn(a, b):
    return lax.dot_general(a, b, (((0,), (0,)), ((), ())), preferred_element_type=jnp.float32)


def on_device(attention_output, frozen_weight, adapter_down, adapter_up, magnitude, cotangent):
    tensor_count = lax.axis_size("tensor")
    tensor_index = lax.axis_index("tensor")
    fsdp_count = lax.axis_size("fsdp")
    fsdp_index = lax.axis_index("fsdp")
    depth = fsdp_count // 4
    x, y, z = fsdp_index % 2, (fsdp_index // 2) % 2, fsdp_index // 4
    tok_rows, in_rows = attention_output.shape
    rank, output_columns = adapter_up.shape
    own_columns = frozen_weight.shape[1]
    block_columns = output_columns // tensor_count
    plane_columns = output_columns // depth
    block_planes = depth // tensor_count
    grad_scale = (tok_rows * fsdp_count) ** (-0.5)

    weight_t = frozen_weight.T
    step = in_rows // len(routes)
    cuts = [(i * step, (i + 1) * step) for i in range(len(routes))]
    gathered = [
        gather_planes(weight_t[:, low:high], route, x, y, z, depth)
        for (low, high), route in zip(cuts, routes)
    ]
    planes = jnp.array([source_plane(i, depth) for i in range(depth)], jnp.int32)
    plane_of = lax.dynamic_index_in_dim(planes, z, 0, keepdims=False)
    positions = jnp.array(
        [[source_plane(i, depth).index(p) for p in range(depth)] for i in range(depth)], jnp.int32
    )
    position_of = lax.dynamic_index_in_dim(positions, z, 0, keepdims=False)

    up_own = lax.dynamic_slice_in_dim(adapter_up, fsdp_index * own_columns, own_columns, 1)
    merged = frozen_weight.astype(jnp.float32) + nn(adapter_down, up_own)
    square_own = sum_over(jnp.sum(merged * merged, axis=0), "tensor")
    square_sum = lax.all_gather(square_own, "fsdp", axis=0, tiled=True)
    col_norms = jnp.sqrt(square_sum + eps_norm)
    col_scale = magnitude / col_norms

    adapter_hidden = sum_over(nn(attention_output, adapter_down), "tensor").astype(jnp.bfloat16)

    gathered_cot = lax.all_gather(cotangent, "tensor", axis=1, tiled=True)
    prescale_gradient = (gathered_cot.astype(jnp.float32) * col_scale[None, :]).astype(jnp.bfloat16)
    lowrank_gradient = nt(prescale_gradient, adapter_up).astype(jnp.bfloat16)
    in_term = tn(attention_output, lowrank_gradient)
    block_offset = tensor_index * block_columns

    def own_block(vector):
        return lax.dynamic_slice_in_dim(vector, block_offset, block_columns, vector.ndim - 1)

    scale_block = own_block(col_scale)
    norms_block = own_block(col_norms)
    magnitude_block = own_block(magnitude)
    grad_block = (cotangent.astype(jnp.float32) * scale_block[None, :]).astype(jnp.bfloat16)
    up_term = tn(adapter_hidden, grad_block)
    in_sum, up_sum = lax.psum((in_term, up_term), "fsdp")

    gradient_planes = jnp.stack(
        [prescale_gradient[:, i * plane_columns : (i + 1) * plane_columns] for i in range(depth)]
    )
    gradient_at = [
        lax.dynamic_index_in_dim(gradient_planes, plane_of[p], 0, keepdims=False)
        for p in range(depth)
    ]

    product = [0.0] * depth
    cross = [0.0] * depth
    gradient_parts = []
    for (low, high), blocks in zip(cuts, gathered):
        rows = attention_output[:, low:high]
        down_rows = adapter_down[low:high]
        running = nt(lowrank_gradient, down_rows)
        for p in range(depth):
            product[p] = product[p] + nt(rows, blocks[p])
            cross[p] = cross[p] + lax.dot_general(
                down_rows, blocks[p], (((0,), (1,)), ((), ())), preferred_element_type=jnp.float32
            )
            running = running + nn(gradient_at[p], blocks[p])
        gradient_parts.append(running.astype(jnp.bfloat16))
    input_gradient = jnp.concatenate(gradient_parts, axis=1)

    def to_blocks(parts):
        stacked = jnp.stack(parts)

        def of_block(index):
            return [
                lax.dynamic_index_in_dim(
                    stacked, position_of[index * block_planes + i], 0, keepdims=False
                )
                for i in range(block_planes)
            ]

        def joined(index):
            return jnp.concatenate(of_block(index), axis=1)

        total = joined(tensor_index).astype(jnp.float32)
        for shift in range(1, tensor_count):
            target = (tensor_index + shift) % tensor_count
            received = lax.ppermute(
                joined(target), "tensor", [(i, (i + shift) % tensor_count) for i in range(tensor_count)]
            )
            total = total + received.astype(jnp.float32)
        return total

    base_block = to_blocks([part.astype(jnp.bfloat16) for part in product])
    pre_block = base_block + nn(adapter_hidden, own_block(adapter_up))
    layer_out = (pre_block * scale_block[None, :]).astype(jnp.bfloat16)
    weighted_sum = sum_over(jnp.sum(cotangent.astype(jnp.float32) * pre_block, axis=0), "fsdp")
    weighted_block = weighted_sum / norms_block
    coef_block = -weighted_block * magnitude_block / (norms_block * norms_block)
    column_coefficient = lax.all_gather(coef_block, "tensor", axis=0, tiled=True)

    scaled_up = (column_coefficient[:, None] * adapter_up.astype(jnp.float32).T).astype(jnp.bfloat16)
    up_inner = nn(adapter_up, scaled_up)
    scaled_planes = scaled_up.reshape(depth, plane_columns, rank)
    scaled_at = [
        lax.dynamic_index_in_dim(scaled_planes, plane_of[p], 0, keepdims=False)
        for p in range(depth)
    ]
    norm_parts = []
    for blocks in gathered:
        running = tn(blocks[0], scaled_at[0])
        for p in range(1, depth):
            running = running + tn(blocks[p], scaled_at[p])
        norm_parts.append(running)
    norm_down = jnp.concatenate(norm_parts, axis=0)
    down_gradient = (
        in_sum
        + norm_down
        + jnp.dot(adapter_down.astype(jnp.float32), up_inner, precision=lax.Precision.HIGHEST)
    ) * grad_scale

    gram = sum_over(tn(adapter_down, adapter_down), "tensor")
    project = to_blocks(cross) + jnp.dot(
        gram, own_block(adapter_up).astype(jnp.float32), precision=lax.Precision.HIGHEST
    )
    d_up = (up_sum + project * coef_block[None, :]) * grad_scale
    d_magnitude = weighted_block * grad_scale
    return (layer_out, input_gradient, down_gradient, d_up, d_magnitude)


def solution(mesh):
    return jax.shard_map(
        on_device,
        mesh=mesh,
        in_specs=(
            P("fsdp", "tensor"),
            P("tensor", "fsdp"),
            P("tensor", None),
            P(),
            P(),
            P("fsdp", "tensor"),
        ),
        out_specs=(
            P("fsdp", "tensor"),
            P("fsdp", "tensor"),
            P("tensor", None),
            P(None, "tensor"),
            P("tensor"),
        ),
        check_vma=False,
    )
```

```python
import functools
import math

import jax
import jax.numpy as jnp
from jax import lax
from jax.experimental import pallas as pl
from jax.experimental.pallas import tpu as pltpu
from jax.sharding import PartitionSpec as P

eps_norm = 1e-06
def flip(value, axis, bit):
    pairs = [(i, i ^ bit) for i in range(lax.axis_size(axis))]
    return lax.ppermute(value, axis, pairs)


def sum_over(value, axis):
    bit = 1
    while bit < lax.axis_size(axis):
        value = value + flip(value, axis, bit)
        bit *= 2
    return value


def arrivals(z, depth):
    found = [("own", 0)]
    for hops in range(1, depth):
        if z - hops >= 0:
            found.append(("up", hops))
        if z + hops < depth:
            found.append(("down", hops))
    return found


def source_plane(z, depth):
    return [z - hops if way == "up" else z + hops for way, hops in arrivals(z, depth)]


def tied(value, *token):
    return lax.optimization_barrier((value, token))[0]


def chosen_by(index, values):
    result = values[0]
    for place, value in enumerate(values):
        if place:
            result = jnp.where(index == place, value, result)
    return result


def nt(a, b):
    return lax.dot_general(a, b, (((1,), (1,)), ((), ())), preferred_element_type=jnp.float32)


def nn(a, b):
    return jnp.dot(a, b, preferred_element_type=jnp.float32)


def tn(a, b):
    return lax.dot_general(a, b, (((0,), (0,)), ((), ())), preferred_element_type=jnp.float32)


no_cost = pl.CostEstimate(flops=0, bytes_accessed=0, transcendentals=0)
in_order = pltpu.CompilerParams(
    dimension_semantics=("arbitrary",), vmem_limit_bytes=24 * 2**20
)


def complete_kernel(parts, *refs):
    refs = list(refs)
    base = refs.pop(0)[...].astype(jnp.float32)
    for _ in range(parts - 1):
        base = base + refs.pop(0)[...].astype(jnp.float32)
    hidden, up, cot, scale, layer, weighted = refs
    pre = base + nn(hidden[...], up[...])
    layer[...] = (pre * scale[...]).astype(jnp.bfloat16)
    weighted[...] = jnp.sum(cot[...].astype(jnp.float32) * pre, axis=0, keepdims=True)


def complete_columns(parts, hidden, up, cot, scale, position):
    height, columns = parts[0].shape
    count = up.shape[1] // columns
    width = columns // 4

    def own(rows):
        return pl.BlockSpec((rows, width), lambda i: (0, i))

    def across(rows):
        return pl.BlockSpec((rows, width), lambda i: (0, position * 4 + i))

    return pl.pallas_call(
        functools.partial(complete_kernel, len(parts)),
        grid=(4,),
        in_specs=[own(height)] * len(parts)
        + [pl.BlockSpec(hidden.shape, lambda i: (0, 0))]
        + [across(up.shape[0]), across(height), across(1)],
        out_specs=[own(height), own(1)],
        out_shape=[
            jax.ShapeDtypeStruct((height, columns), jnp.bfloat16),
            jax.ShapeDtypeStruct((1, columns), jnp.float32),
        ],
        compiler_params=in_order,
        cost_estimate=no_cost,
    )(*parts, hidden, up, cot, scale)


def assemble_kernel(cases, index, *refs):
    out, semaphore = refs[-2], refs[-1]
    for case, copies in enumerate(cases):

        @pl.when(index[0] == case)
        def _(copies=copies):
            started = []
            for number, (source, part, place) in enumerate(copies):
                copy = pltpu.make_async_copy(
                    refs[source].at[part], out.at[place], semaphore.at[number]
                )
                copy.start()
                started.append(copy)
            for copy in started:
                copy.wait()


def assemble(index, cases, arrays, shape):
    size = 2 * math.prod(shape)
    return pl.pallas_call(
        functools.partial(assemble_kernel, cases),
        in_specs=[pl.BlockSpec(memory_space=pltpu.SMEM)]
        + [pl.BlockSpec(memory_space=pl.ANY)] * len(arrays),
        out_specs=pl.BlockSpec(memory_space=pltpu.VMEM),
        out_shape=jax.ShapeDtypeStruct(shape, arrays[0].dtype),
        scratch_shapes=[pltpu.SemaphoreType.DMA((len(cases[0]),))],
        compiler_params=pltpu.CompilerParams(vmem_limit_bytes=2 * size + 4 * 2**20),
        cost_estimate=no_cost,
    )(index.reshape(1), *arrays)


def reordered_kernel(width, places, source, out):
    for place in range(out.shape[1] // width):
        start = pl.multiple_of(places[place] * width, width)
        out[:, place * width : (place + 1) * width] = source[:, pl.ds(start, width)]


def reordered(matrix, places, width):
    shape = (matrix.shape[0], places.shape[0] * width)
    return pl.pallas_call(
        functools.partial(reordered_kernel, width),
        in_specs=[
            pl.BlockSpec(memory_space=pltpu.SMEM),
            pl.BlockSpec(memory_space=pltpu.VMEM),
        ],
        out_specs=pl.BlockSpec(memory_space=pltpu.VMEM),
        out_shape=jax.ShapeDtypeStruct(shape, matrix.dtype),
        compiler_params=pltpu.CompilerParams(vmem_limit_bytes=24 * 2**20),
        cost_estimate=no_cost,
    )(places, matrix)


def on_device(attention_output, frozen_weight, adapter_down, adapter_up, magnitude, cotangent):
    tensor_count = lax.axis_size("tensor")
    tensor_index = lax.axis_index("tensor")
    fsdp_count = lax.axis_size("fsdp")
    fsdp_index = lax.axis_index("fsdp")
    depth = fsdp_count // 4
    x, y, z = fsdp_index % 2, (fsdp_index // 2) % 2, fsdp_index // 4
    tok_rows, in_rows = attention_output.shape
    rank, output_columns = adapter_up.shape
    own_columns = frozen_weight.shape[1]
    block_columns = output_columns // tensor_count
    plane_columns = output_columns // depth
    block_planes = depth // tensor_count
    grad_scale = (tok_rows * fsdp_count) ** (-0.5)
    across_x = [(i, i ^ 1) for i in range(fsdp_count)]
    across_y = [(i, i ^ 2) for i in range(fsdp_count)]
    z_bits = [1 << i for i in range(2, fsdp_count.bit_length() - 1)]
    planes = chosen_by(
        z, [jnp.array(source_plane(i, depth), jnp.int32)[:, None] for i in range(depth)]
    )
    slots = jnp.arange(4, dtype=jnp.int32)
    owner_of = (4 * planes + 2 * (y ^ (slots // 2)) + (x ^ (slots % 2))).reshape(-1)
    positions = chosen_by(
        z,
        [
            jnp.array([source_plane(i, depth).index(p) for p in range(depth)], jnp.int32)[:, None]
            for i in range(depth)
        ],
    )
    slot_of = (4 * positions + 2 * (y ^ (slots // 2)) + (x ^ (slots % 2))).reshape(-1)
    own_owners = fsdp_count // tensor_count
    own_slots = chosen_by(
        tensor_index, [slot_of[i * own_owners : (i + 1) * own_owners] for i in range(tensor_count)]
    )
    block_offset = tensor_index * block_columns

    def own_block(vector):
        return lax.dynamic_slice_in_dim(vector, block_offset, block_columns, vector.ndim - 1)

    up_own = lax.dynamic_slice_in_dim(adapter_up, fsdp_index * own_columns, own_columns, 1)
    merged = frozen_weight.astype(jnp.float32) + nn(adapter_down, up_own)
    square_own = sum_over(jnp.sum(merged * merged, axis=0), "tensor")

    adapter_hidden = sum_over(nn(attention_output, adapter_down), "tensor").astype(jnp.bfloat16)
    cot_slots = reordered(
        lax.all_gather(cotangent, "tensor", axis=1, tiled=True), owner_of, own_columns
    )
    up_slots = reordered(adapter_up, owner_of, own_columns)
    gram = sum_over(tn(adapter_down, adapter_down), "tensor")

    weight_t = frozen_weight.T
    half = in_rows // 2
    here = jnp.zeros((), jnp.int32)
    all_lanes = slice(None)
    lanes = {"c": slice(0, half), "d": slice(half, in_rows)}

    class Lane:
        def __init__(self, pairs):
            self.pairs = pairs
            self.results = []

        def send(self, value, *before):
            value = tied(value, tuple(self.results[-2:-1]), before)
            self.results.append(lax.ppermute(value, "fsdp", self.pairs))
            return self.results[-1]

    lane_x, lane_y = Lane(across_x), Lane(across_y)

    def side(bit):
        return (fsdp_index // bit) % 2 == 0

    def widen(value, bit, *token):
        other = flip(tied(value, *token), "fsdp", bit)
        return jnp.concatenate(
            [jnp.where(side(bit), value, other), jnp.where(side(bit), other, value)], axis=-1
        )

    def halve(value, bit, *token):
        middle = value.shape[-1] // 2
        low, high = value[..., :middle], value[..., middle:]
        mine = tied(jnp.where(side(bit), high, low).astype(jnp.bfloat16), *token)
        moved = flip(mine, "fsdp", bit)
        return jnp.where(side(bit), low, high) + moved.astype(jnp.float32)

    def add(value, bit, *token):
        value = tied(value.astype(jnp.bfloat16), *token)
        return (value.astype(jnp.float32) + flip(value, "fsdp", bit).astype(jnp.float32)).astype(
            jnp.bfloat16
        )

    held = {("own", 0): weight_t, ("up", 0): weight_t, ("down", 0): weight_t}

    def send_z(hops, *before):
        held["up", hops] = lax.ppermute(
            tied(held["up", hops - 1], *before),
            "fsdp",
            [(i, i + 4) for i in range(fsdp_count - 4) if i // 4 >= hops - 1],
        )
        held["down", hops] = lax.ppermute(
            tied(held["down", hops - 1], *before),
            "fsdp",
            [(i, i - 4) for i in range(4, fsdp_count) if i // 4 + hops - 1 < depth],
        )
        return held["up", hops], held["down", hops]

    def own_block_at(name, position):
        wanted = [arrivals(plane, depth)[position] for plane in range(depth)]
        sources = sorted(set(wanted))
        cases = [[(sources.index(w), (all_lanes, lanes[name]), (0,))] for w in wanted]
        return assemble(z, cases, [held[w] for w in sources], (1, own_columns, half))

    blocks = {}
    quads = {}

    def start_turn(number, *before):
        position, turn = divmod(number, 3)
        if turn == 0:
            for name in "cd":
                blocks[name, position] = [own_block_at(name, position)]
        for name, lane in (("cdd"[turn], lane_x), ("dcc"[turn], lane_y)):
            source = blocks[name, position][1 if turn == 2 else 0]
            blocks[name, position].append(lane.send(source, *before))

    def finish(position):
        copies = []
        for name, slots in (("c", (0, 1, 2, 3)), ("d", (0, 2, 1, 3))):
            for slot in slots:
                copies.append((len(copies), (0,), (slot, all_lanes, lanes[name])))
        sources = blocks["c", position] + blocks["d", position]
        quad = assemble(here, [copies], sources, (4, own_columns, in_rows))
        quads[position] = quad.reshape(plane_columns, in_rows)

    cross = [None] * depth
    layer_parts = [None] * depth
    weighted_parts = [None] * depth
    exchanged = [None] * depth
    running = None

    def across_cores(mine):
        return [mine] + [
            lax.ppermute(
                mine, "tensor", [(i, (i + shift) % tensor_count) for i in range(tensor_count)]
            )
            for shift in range(1, tensor_count)
        ]

    def columns_at(matrix, position):
        return matrix[:, position * plane_columns : (position + 1) * plane_columns]

    def forward(position):
        finish(position)
        product = nt(attention_output, quads[position]).astype(jnp.bfloat16)
        exchanged[position] = across_cores(product)
        cross[position] = nt(down_t, quads[position])
        return (product,)

    def complete(position):
        layer_parts[position], weighted_parts[position] = complete_columns(
            exchanged[position], adapter_hidden, up_slots, cot_slots, scale_slots, position
        )
        return layer_parts[position], weighted_parts[position]

    def backward(position):
        nonlocal running
        running = running + nn(columns_at(gradient_slots, position), quads[position])
        return (running,)

    down_t = adapter_down.T
    start_turn(0)
    start_turn(1)
    arrived_z = send_z(1)
    squares = widen(square_own, 1)
    start_turn(2)
    squares = widen(squares, 2, blocks["d", 0][1])
    start_turn(3, squares)
    arrived_z = send_z(2, arrived_z)
    for bit in z_bits:
        squares = widen(squares, bit, arrived_z)
    for hops in range(3, depth):
        arrived_z = send_z(hops, arrived_z, squares)

    col_norms = jnp.sqrt(squares + eps_norm)
    col_scale = magnitude / col_norms
    scale_slots = reordered(col_scale[None, :], owner_of, own_columns)
    gradient_slots = (cot_slots.astype(jnp.float32) * scale_slots).astype(jnp.bfloat16)
    lowrank_gradient = nt(gradient_slots, up_slots).astype(jnp.bfloat16)
    scale_block = own_block(col_scale)
    grad_block = (cotangent.astype(jnp.float32) * scale_block[None, :]).astype(jnp.bfloat16)
    sums = jnp.concatenate(
        [tn(lowrank_gradient, attention_output), tn(adapter_hidden, grad_block)], axis=1
    )
    running = nn(lowrank_gradient, down_t)

    start_turn(4)
    work = forward(0)
    start_turn(5, work)
    work = (sums, gradient_slots, running)
    for bit in z_bits:
        sums = halve(sums, bit, arrived_z)
    for number in range(6, 3 * depth):
        position, turn = divmod(number, 3)
        if turn == 0:
            work += backward(position - 2) + complete(position - 2)
        start_turn(number, work)
        work = ()
        if turn == 1:
            work = forward(position - 1)
        if number == 3 * depth - 5:
            sums = add(sums, 1, lane_x.results[-2])
        if number == 3 * depth - 3:
            sums = add(sums, 2, lane_y.results[-2])
    work = backward(depth - 2) + complete(depth - 2)
    for bit in reversed(z_bits):
        sums = widen(sums, bit)
    in_sum = sums[:, :in_rows].astype(jnp.float32)
    up_sum = sums[:, in_rows:].astype(jnp.float32)

    forward(depth - 1)
    complete(depth - 1)
    input_gradient = backward(depth - 1)[0].astype(jnp.bfloat16)

    layer_out = reordered(jnp.concatenate(layer_parts, axis=1), own_slots, own_columns)

    weighted_sum = sum_over(
        reordered(jnp.concatenate(weighted_parts, axis=1), slot_of, own_columns)[0], "fsdp"
    )
    weighted = weighted_sum / col_norms
    coef = -weighted * magnitude / (col_norms * col_norms)
    scaled_up = (adapter_up.astype(jnp.float32) * coef[None, :]).astype(jnp.bfloat16)
    up_inner = nt(scaled_up, adapter_up)
    scaled_slots = reordered(scaled_up, owner_of, own_columns)
    norm_down = nn(columns_at(scaled_slots, 0), quads[0])
    for position in range(1, depth):
        norm_down = norm_down + nn(columns_at(scaled_slots, position), quads[position])
    inner_down = lax.dot_general(
        up_inner,
        adapter_down.astype(jnp.float32),
        (((1,), (1,)), ((), ())),
        precision=lax.Precision.HIGHEST,
    )
    down_gradient = ((in_sum + norm_down + inner_down) * grad_scale).T
    crossed = across_cores(jnp.concatenate(cross, axis=1))
    project = reordered(sum(crossed[1:], crossed[0]), own_slots, own_columns) + jnp.dot(
        gram, own_block(adapter_up).astype(jnp.float32), precision=lax.Precision.HIGHEST
    )
    d_up = (up_sum + project * own_block(coef)[None, :]) * grad_scale
    d_magnitude = own_block(weighted) * grad_scale
    return (layer_out, input_gradient, down_gradient, d_up, d_magnitude)


def solution(mesh):
    return jax.shard_map(
        on_device,
        mesh=mesh,
        in_specs=(
            P("fsdp", "tensor"),
            P("tensor", "fsdp"),
            P("tensor", None),
            P(),
            P(),
            P("fsdp", "tensor"),
        ),
        out_specs=(
            P("fsdp", "tensor"),
            P("fsdp", "tensor"),
            P("tensor", None),
            P(None, "tensor"),
            P("tensor"),
        ),
        check_vma=False,
    )
```

```python
import functools
import math

import jax
import jax.numpy as jnp
from jax import lax
from jax.experimental import pallas as pl
from jax.experimental.pallas import tpu as pltpu
from jax.sharding import PartitionSpec as P

eps_norm = 1e-06
def flip(value, axis, bit):
    pairs = [(i, i ^ bit) for i in range(lax.axis_size(axis))]
    return lax.ppermute(value, axis, pairs)


def sum_over(value, axis):
    bit = 1
    while bit < lax.axis_size(axis):
        value = value + flip(value, axis, bit)
        bit *= 2
    return value


def arrivals(z, depth):
    found = [("own", 0)]
    for hops in range(1, depth):
        if z - hops >= 0:
            found.append(("up", hops))
        if z + hops < depth:
            found.append(("down", hops))
    return found


def source_plane(z, depth):
    return [z - hops if way == "up" else z + hops for way, hops in arrivals(z, depth)]


def tied(value, *token):
    return lax.optimization_barrier((value, token))[0]


def chosen_by(index, values):
    result = values[0]
    for place, value in enumerate(values):
        if place:
            result = jnp.where(index == place, value, result)
    return result


def nt(a, b):
    return lax.dot_general(a, b, (((1,), (1,)), ((), ())), preferred_element_type=jnp.float32)


def nn(a, b):
    return jnp.dot(a, b, preferred_element_type=jnp.float32)


def tn(a, b):
    return lax.dot_general(a, b, (((0,), (0,)), ((), ())), preferred_element_type=jnp.float32)


no_cost = pl.CostEstimate(flops=0, bytes_accessed=0, transcendentals=0)
in_order = pltpu.CompilerParams(
    dimension_semantics=("arbitrary",), vmem_limit_bytes=24 * 2**20
)


def complete_kernel(parts, *refs):
    refs = list(refs)
    base = refs.pop(0)[...].astype(jnp.float32)
    for _ in range(parts - 1):
        base = base + refs.pop(0)[...].astype(jnp.float32)
    hidden, up, cot, scale, layer, weighted = refs
    pre = base + nn(hidden[...], up[...])
    layer[...] = (pre * scale[...]).astype(jnp.bfloat16)
    weighted[...] = jnp.sum(cot[...].astype(jnp.float32) * pre, axis=0, keepdims=True)


def complete_columns(parts, hidden, up, cot, scale, first, width):
    height, columns = parts[0].shape

    def own(rows):
        return pl.BlockSpec((rows, width), lambda i: (0, i))

    def across(rows):
        return pl.BlockSpec((rows, width), lambda i: (0, first + i))

    return pl.pallas_call(
        functools.partial(complete_kernel, len(parts)),
        grid=(columns // width,),
        in_specs=[own(height)] * len(parts)
        + [pl.BlockSpec(hidden.shape, lambda i: (0, 0))]
        + [across(up.shape[0]), across(height), across(1)],
        out_specs=[own(height), own(1)],
        out_shape=[
            jax.ShapeDtypeStruct((height, columns), jnp.bfloat16),
            jax.ShapeDtypeStruct((1, columns), jnp.float32),
        ],
        compiler_params=in_order,
        cost_estimate=no_cost,
    )(*parts, hidden, up, cot, scale)


def gradient_kernel(count, *refs):
    total = refs[2 * count][...]
    for number in range(count):
        total += nn(refs[number][...], refs[count + number][...])
    refs[-1][...] = total.astype(jnp.bfloat16)


def last_gradient(gradients, weights, before):
    height, depth = before.shape
    lanes = min(depth, 512)
    across = pl.BlockSpec((height, lanes), lambda i: (0, i))
    return pl.pallas_call(
        functools.partial(gradient_kernel, len(weights)),
        grid=(depth // lanes,),
        in_specs=[pl.BlockSpec(value.shape, lambda i: (0, 0)) for value in gradients]
        + [pl.BlockSpec((value.shape[0], lanes), lambda i: (0, i)) for value in weights]
        + [across],
        out_specs=across,
        out_shape=jax.ShapeDtypeStruct(before.shape, jnp.bfloat16),
        compiler_params=in_order,
        cost_estimate=no_cost,
    )(*gradients, *weights, before)


def assemble_kernel(cases, index, *refs):
    out, semaphore = refs[-2], refs[-1]
    for case, copies in enumerate(cases):

        @pl.when(index[0] == case)
        def _(copies=copies):
            started = []
            for number, (source, part, place) in enumerate(copies):
                copy = pltpu.make_async_copy(
                    refs[source].at[part], out.at[place], semaphore.at[number]
                )
                copy.start()
                started.append(copy)
            for copy in started:
                copy.wait()


def assemble(index, cases, arrays, shape):
    size = 2 * math.prod(shape)
    return pl.pallas_call(
        functools.partial(assemble_kernel, cases),
        in_specs=[pl.BlockSpec(memory_space=pltpu.SMEM)]
        + [pl.BlockSpec(memory_space=pl.ANY)] * len(arrays),
        out_specs=pl.BlockSpec(memory_space=pltpu.VMEM),
        out_shape=jax.ShapeDtypeStruct(shape, arrays[0].dtype),
        scratch_shapes=[pltpu.SemaphoreType.DMA((len(cases[0]),))],
        compiler_params=pltpu.CompilerParams(vmem_limit_bytes=2 * size + 4 * 2**20),
        cost_estimate=no_cost,
    )(index.reshape(1), *arrays)


def reordered_kernel(width, places, source, out):
    for place in range(out.shape[1] // width):
        start = pl.multiple_of(places[place] * width, width)
        out[:, place * width : (place + 1) * width] = source[:, pl.ds(start, width)]


def reordered(matrix, places, width):
    shape = (matrix.shape[0], places.shape[0] * width)
    return pl.pallas_call(
        functools.partial(reordered_kernel, width),
        in_specs=[
            pl.BlockSpec(memory_space=pltpu.SMEM),
            pl.BlockSpec(memory_space=pltpu.VMEM),
        ],
        out_specs=pl.BlockSpec(memory_space=pltpu.VMEM),
        out_shape=jax.ShapeDtypeStruct(shape, matrix.dtype),
        compiler_params=pltpu.CompilerParams(vmem_limit_bytes=24 * 2**20),
        cost_estimate=no_cost,
    )(places, matrix)


def on_device(attention_output, frozen_weight, adapter_down, adapter_up, magnitude, cotangent):
    tensor_count = lax.axis_size("tensor")
    tensor_index = lax.axis_index("tensor")
    fsdp_count = lax.axis_size("fsdp")
    fsdp_index = lax.axis_index("fsdp")
    depth = fsdp_count // 4
    x, y, z = fsdp_index % 2, (fsdp_index // 2) % 2, fsdp_index // 4
    tok_rows, in_rows = attention_output.shape
    rank, output_columns = adapter_up.shape
    own_columns = frozen_weight.shape[1]
    block_columns = output_columns // tensor_count
    plane_columns = output_columns // depth
    block_planes = depth // tensor_count
    grad_scale = (tok_rows * fsdp_count) ** (-0.5)
    across_x = [(i, i ^ 1) for i in range(fsdp_count)]
    across_y = [(i, i ^ 2) for i in range(fsdp_count)]
    z_bits = [1 << i for i in range(2, fsdp_count.bit_length() - 1)]
    planes = chosen_by(
        z, [jnp.array(source_plane(i, depth), jnp.int32)[:, None] for i in range(depth)]
    )
    slots = jnp.arange(4, dtype=jnp.int32)
    owner_of = (4 * planes + 2 * (y ^ (slots // 2)) + (x ^ (slots % 2))).reshape(-1)
    positions = chosen_by(
        z,
        [
            jnp.array([source_plane(i, depth).index(p) for p in range(depth)], jnp.int32)[:, None]
            for i in range(depth)
        ],
    )
    slot_of = (4 * positions + 2 * (y ^ (slots // 2)) + (x ^ (slots % 2))).reshape(-1)
    own_owners = fsdp_count // tensor_count
    own_slots = chosen_by(
        tensor_index, [slot_of[i * own_owners : (i + 1) * own_owners] for i in range(tensor_count)]
    )
    block_offset = tensor_index * block_columns

    def own_block(vector):
        return lax.dynamic_slice_in_dim(vector, block_offset, block_columns, vector.ndim - 1)

    up_own = lax.dynamic_slice_in_dim(adapter_up, fsdp_index * own_columns, own_columns, 1)
    merged = frozen_weight.astype(jnp.float32) + nn(adapter_down, up_own)
    square_own = sum_over(jnp.sum(merged * merged, axis=0), "tensor")

    adapter_hidden = sum_over(nn(attention_output, adapter_down), "tensor").astype(jnp.bfloat16)
    cot_slots = reordered(
        lax.all_gather(cotangent, "tensor", axis=1, tiled=True), owner_of, own_columns
    )
    up_slots = reordered(adapter_up, owner_of, own_columns)
    gram = sum_over(tn(adapter_down, adapter_down), "tensor")

    half = in_rows // 2
    here = jnp.zeros((), jnp.int32)
    all_lanes = slice(None)
    lanes = {"c": slice(0, half), "d": slice(half, in_rows)}
    down_t = adapter_down.T

    def side(bit):
        return (fsdp_index // bit) % 2 == 0

    def widen(value, bit, *token):
        other = flip(tied(value, *token), "fsdp", bit)
        return jnp.concatenate(
            [jnp.where(side(bit), value, other), jnp.where(side(bit), other, value)], axis=-1
        )

    def halve(value, bit, *token):
        middle = value.shape[-1] // 2
        low, high = value[..., :middle], value[..., middle:]
        mine = tied(jnp.where(side(bit), high, low).astype(jnp.bfloat16), *token)
        moved = flip(mine, "fsdp", bit)
        return jnp.where(side(bit), low, high) + moved.astype(jnp.float32)

    def add(value, bit, *token):
        value = tied(value.astype(jnp.bfloat16), *token)
        return (value.astype(jnp.float32) + flip(value, "fsdp", bit).astype(jnp.float32)).astype(
            jnp.bfloat16
        )

    held = {(way, 0): frozen_weight.T for way in ("own", "up", "down")}

    def send_z(hops, *before):
        held["up", hops] = lax.ppermute(
            tied(held["up", hops - 1], *before),
            "fsdp",
            [(i, i + 4) for i in range(fsdp_count - 4) if i // 4 >= hops - 1],
        )
        held["down", hops] = lax.ppermute(
            tied(held["down", hops - 1], *before),
            "fsdp",
            [(i, i - 4) for i in range(4, fsdp_count) if i // 4 + hops - 1 < depth],
        )
        return held["up", hops], held["down", hops]

    def own_block_at(position):
        if position == 0:
            return held["own", 0]
        wanted = [arrivals(plane, depth)[position] for plane in range(depth)]
        sources = sorted(set(wanted))
        cases = [[(sources.index(w), all_lanes, all_lanes)] for w in wanted]
        return assemble(z, cases, [held[w] for w in sources], (own_columns, in_rows))

    finished = []
    running = None

    def across_cores(mine):
        return [mine] + [
            lax.ppermute(
                mine, "tensor", [(i, (i + shift) % tensor_count) for i in range(tensor_count)]
            )
            for shift in range(1, tensor_count)
        ]

    class Columns:
        def __init__(self, copies, sources, slots):
            self.slots = slots
            shape = (len(slots) * own_columns, in_rows)
            self.weight = assemble(here, [copies], sources, shape)
            finished.append(self)

        def of(self, matrix):
            parts = [matrix[:, slot * own_columns : (slot + 1) * own_columns] for slot in self.slots]
            return jnp.concatenate(parts, axis=1)

        def forward(self, *token):
            weight = tied(self.weight, *token)
            product = nt(attention_output, weight).astype(jnp.bfloat16)
            self.exchanged = across_cores(product)
            self.cross = nt(down_t, weight)
            return (*self.exchanged, self.cross)

        def complete(self):
            made = complete_columns(
                self.exchanged,
                adapter_hidden,
                self.of(up_slots),
                self.of(cot_slots),
                self.of(scale_slots),
                0,
                own_columns,
            )
            self.layer, self.weighted = made
            return tuple(made)

        def backward(self, *token):
            nonlocal running
            weight = tied(self.weight, *token)
            running = tied(running + nn(self.of(gradient_slots), weight))
            return (running,)

    def near(position):
        sources = [own[position], over_x[position], over_y[position]]
        copies = [
            (i, all_lanes, (slice(i * own_columns, (i + 1) * own_columns), all_lanes))
            for i in range(3)
        ]
        return Columns(copies, sources, [4 * position + i for i in range(3)])

    def far(which):
        copies, sources, slots = [], [], []
        for number, position in enumerate(which):
            for name, (got, part) in zip("cd", ends[position]):
                copies.append(
                    (
                        len(sources),
                        slice(part * own_columns, (part + 1) * own_columns),
                        (slice(number * own_columns, (number + 1) * own_columns), lanes[name]),
                    )
                )
                sources.append(got)
            slots.append(4 * position + 3)
        return Columns(copies, sources, slots)

    def start_far(which, *before):
        halves = []
        for name, came in (("d", over_y), ("c", over_x)):
            sources = [came[position] for position in which]
            copies = [
                (i, (all_lanes, lanes[name]), slice(i * own_columns, (i + 1) * own_columns))
                for i in range(len(which))
            ]
            shape = (len(which) * own_columns, half)
            halves.append(tied(assemble(here, [copies], sources, shape), *before))
        got_d = lax.ppermute(halves[0], "fsdp", across_x)
        got_c = lax.ppermute(halves[1], "fsdp", across_y)
        for number, position in enumerate(which):
            ends[position] = ((got_c, number), (got_d, number))
        return got_c, got_d

    turns = [("near", [position]) for position in range(depth)]
    turns += [("far", list(range(depth - 2))), ("far", [depth - 2]), ("far", [depth - 1])]
    norms_turn = depth - 1
    own, over_x, over_y, ends = {}, {}, {}, {}
    squares = square_own
    token = work = ()
    arrived = []
    waiting = []
    for number, (kind, which) in enumerate(turns):
        before = (token, work)
        token = ()
        work = ()
        if kind == "near":
            position = which[0]
            own[position] = block = tied(own_block_at(position), *before)
            over_x[position] = lax.ppermute(block, "fsdp", across_x)
            over_y[position] = lax.ppermute(block, "fsdp", across_y)
            token += (over_x[position], over_y[position])
            if position + 1 < depth:
                token += send_z(position + 1, *before)
        else:
            token += start_far(which, *before)

        if number < 2:
            squares = widen(squares, (1, 2)[number], *before)
            work += (squares,)
        if number == norms_turn:
            for bit in z_bits:
                squares = widen(squares, bit, *before)
        if number == norms_turn:
            col_norms = jnp.sqrt(squares + eps_norm)
            col_scale = magnitude / col_norms
            scale_slots = reordered(col_scale[None, :], owner_of, own_columns)
            gradient_slots = (cot_slots.astype(jnp.float32) * scale_slots).astype(jnp.bfloat16)
            lowrank_gradient = nt(gradient_slots, up_slots).astype(jnp.bfloat16)
            scale_block = own_block(col_scale)
            grad_block = (cotangent.astype(jnp.float32) * scale_block[None, :]).astype(jnp.bfloat16)
            sums = jnp.concatenate(
                [tn(lowrank_gradient, attention_output), tn(adapter_hidden, grad_block)], axis=1
            )
            running = nn(lowrank_gradient, down_t)
            work += (sums, running)
        if number == norms_turn + 1:
            for bit in z_bits:
                sums = halve(sums, bit, before)
            sums = add(sums, 1)
            work += (sums,)
        if number == norms_turn + 2:
            sums = add(sums, 2, before)
            work += (sums,)
        if number == norms_turn + 3:
            for bit in reversed(z_bits):
                sums = widen(sums, bit, before)

        for columns in arrived:
            work += columns.forward(before)
            waiting.append(columns)
        arrived = [near(which[0]) if kind == "near" else far(which)]
        if number > norms_turn:
            for columns in waiting[: 1 + (number == len(turns) - 1)]:
                work += columns.backward(before) + columns.complete()
            waiting = waiting[1 + (number == len(turns) - 1) :]
    in_sum = sums[:, :in_rows].astype(jnp.float32)
    up_sum = sums[:, in_rows:].astype(jnp.float32)

    for columns in arrived:
        columns.forward(token)
        waiting.append(columns)
    for columns in waiting:
        columns.complete()
    input_gradient = last_gradient(
        [columns.of(gradient_slots) for columns in waiting],
        [columns.weight for columns in waiting],
        running,
    )
    order = [slot for columns in finished for slot in columns.slots]
    place = jnp.array([order.index(slot) for slot in range(fsdp_count)], jnp.int32)

    def joined_columns(parts, places):
        return reordered(jnp.concatenate(parts, axis=1), place[places], own_columns)

    layer_out = joined_columns([columns.layer for columns in finished], own_slots)

    weighted_parts = [columns.weighted for columns in finished]
    weighted_sum = sum_over(joined_columns(weighted_parts, slot_of)[0], "fsdp")
    weighted = weighted_sum / col_norms
    coef = -weighted * magnitude / (col_norms * col_norms)
    scaled_up = (adapter_up.astype(jnp.float32) * coef[None, :]).astype(jnp.bfloat16)
    up_inner = nt(scaled_up, adapter_up)
    scaled_slots = reordered(scaled_up, owner_of, own_columns)
    norm_down = sum(nn(part.of(scaled_slots), part.weight) for part in finished)
    inner_down = lax.dot_general(
        up_inner,
        adapter_down.astype(jnp.float32),
        (((1,), (1,)), ((), ())),
        precision=lax.Precision.HIGHEST,
    )
    down_gradient = ((in_sum + norm_down + inner_down) * grad_scale).T
    crossed = across_cores(jnp.concatenate([columns.cross for columns in finished], axis=1))
    project = joined_columns([sum(crossed[1:], crossed[0])], own_slots) + jnp.dot(
        gram, own_block(adapter_up).astype(jnp.float32), precision=lax.Precision.HIGHEST
    )
    d_up = (up_sum + project * own_block(coef)[None, :]) * grad_scale
    d_magnitude = own_block(weighted) * grad_scale
    return (layer_out, input_gradient, down_gradient, d_up, d_magnitude)


def solution(mesh):
    return jax.shard_map(
        on_device,
        mesh=mesh,
        in_specs=(
            P("fsdp", "tensor"),
            P("tensor", "fsdp"),
            P("tensor", None),
            P(),
            P(),
            P("fsdp", "tensor"),
        ),
        out_specs=(
            P("fsdp", "tensor"),
            P("fsdp", "tensor"),
            P("tensor", None),
            P(None, "tensor"),
            P("tensor"),
        ),
        check_vma=False,
    )
```

```python
import functools
import math

import jax
import jax.numpy as jnp
from jax import lax
from jax.experimental import pallas as pl
from jax.experimental.pallas import tpu as pltpu
from jax.sharding import PartitionSpec as P

eps_norm = 1e-06
def flip(value, axis, bit):
    pairs = [(i, i ^ bit) for i in range(lax.axis_size(axis))]
    return lax.ppermute(value, axis, pairs)


def sum_over(value, axis):
    bit = 1
    while bit < lax.axis_size(axis):
        value = value + flip(value, axis, bit)
        bit *= 2
    return value


def arrivals(z, depth):
    found = [("own", 0)]
    for hops in range(1, depth):
        if z - hops >= 0:
            found.append(("up", hops))
        if z + hops < depth:
            found.append(("down", hops))
    return found


def source_plane(z, depth):
    return [z - hops if way == "up" else z + hops for way, hops in arrivals(z, depth)]


def tied(value, *token):
    return lax.optimization_barrier((value, token))[0]


def chosen_by(index, values):
    result = values[0]
    for place, value in enumerate(values):
        if place:
            result = jnp.where(index == place, value, result)
    return result


def nt(a, b):
    return lax.dot_general(a, b, (((1,), (1,)), ((), ())), preferred_element_type=jnp.float32)


def nn(a, b):
    return jnp.dot(a, b, preferred_element_type=jnp.float32)


def tn(a, b):
    return lax.dot_general(a, b, (((0,), (0,)), ((), ())), preferred_element_type=jnp.float32)


no_cost = pl.CostEstimate(flops=0, bytes_accessed=0, transcendentals=0)
in_order = pltpu.CompilerParams(
    dimension_semantics=("arbitrary",), vmem_limit_bytes=24 * 2**20
)


def complete_kernel(parts, *refs):
    refs = list(refs)
    base = refs.pop(0)[...].astype(jnp.float32)
    for _ in range(parts - 1):
        base = base + refs.pop(0)[...].astype(jnp.float32)
    hidden, up, cot, scale, layer, weighted = refs
    pre = base + nn(hidden[...], up[...])
    layer[...] = (pre * scale[...]).astype(jnp.bfloat16)
    weighted[...] = jnp.sum(cot[...].astype(jnp.float32) * pre, axis=0, keepdims=True)


def complete_columns(parts, hidden, up, cot, scale, first, width):
    height, columns = parts[0].shape

    def own(rows):
        return pl.BlockSpec((rows, width), lambda i: (0, i))

    def across(rows):
        return pl.BlockSpec((rows, width), lambda i: (0, first + i))

    return pl.pallas_call(
        functools.partial(complete_kernel, len(parts)),
        grid=(columns // width,),
        in_specs=[own(height)] * len(parts)
        + [pl.BlockSpec(hidden.shape, lambda i: (0, 0))]
        + [across(up.shape[0]), across(height), across(1)],
        out_specs=[own(height), own(1)],
        out_shape=[
            jax.ShapeDtypeStruct((height, columns), jnp.bfloat16),
            jax.ShapeDtypeStruct((1, columns), jnp.float32),
        ],
        compiler_params=in_order,
        cost_estimate=no_cost,
    )(*parts, hidden, up, cot, scale)


def gradient_kernel(count, *refs):
    total = refs[2 * count][...]
    for number in range(count):
        total += nn(refs[number][...], refs[count + number][...])
    refs[-1][...] = total.astype(jnp.bfloat16)


def last_gradient(gradients, weights, before):
    height, depth = before.shape
    lanes = min(depth, 512)
    across = pl.BlockSpec((height, lanes), lambda i: (0, i))
    return pl.pallas_call(
        functools.partial(gradient_kernel, len(weights)),
        grid=(depth // lanes,),
        in_specs=[pl.BlockSpec(value.shape, lambda i: (0, 0)) for value in gradients]
        + [pl.BlockSpec((value.shape[0], lanes), lambda i: (0, i)) for value in weights]
        + [across],
        out_specs=across,
        out_shape=jax.ShapeDtypeStruct(before.shape, jnp.bfloat16),
        compiler_params=in_order,
        cost_estimate=no_cost,
    )(*gradients, *weights, before)


def assemble_kernel(cases, index, *refs):
    out, semaphore = refs[-2], refs[-1]
    for case, copies in enumerate(cases):

        @pl.when(index[0] == case)
        def _(copies=copies):
            started = []
            for number, (source, part, place) in enumerate(copies):
                copy = pltpu.make_async_copy(
                    refs[source].at[part], out.at[place], semaphore.at[number]
                )
                copy.start()
                started.append(copy)
            for copy in started:
                copy.wait()


def assemble(index, cases, arrays, shape):
    size = 2 * math.prod(shape)
    return pl.pallas_call(
        functools.partial(assemble_kernel, cases),
        in_specs=[pl.BlockSpec(memory_space=pltpu.SMEM)]
        + [pl.BlockSpec(memory_space=pl.ANY)] * len(arrays),
        out_specs=pl.BlockSpec(memory_space=pltpu.VMEM),
        out_shape=jax.ShapeDtypeStruct(shape, arrays[0].dtype),
        scratch_shapes=[pltpu.SemaphoreType.DMA((len(cases[0]),))],
        compiler_params=pltpu.CompilerParams(vmem_limit_bytes=2 * size + 4 * 2**20),
        cost_estimate=no_cost,
    )(index.reshape(1), *arrays)


def reordered_kernel(width, places, source, out):
    for place in range(out.shape[1] // width):
        start = pl.multiple_of(places[place] * width, width)
        out[:, place * width : (place + 1) * width] = source[:, pl.ds(start, width)]


def reordered(matrix, places, width):
    shape = (matrix.shape[0], places.shape[0] * width)
    return pl.pallas_call(
        functools.partial(reordered_kernel, width),
        in_specs=[
            pl.BlockSpec(memory_space=pltpu.SMEM),
            pl.BlockSpec(memory_space=pltpu.VMEM),
        ],
        out_specs=pl.BlockSpec(memory_space=pltpu.VMEM),
        out_shape=jax.ShapeDtypeStruct(shape, matrix.dtype),
        compiler_params=pltpu.CompilerParams(vmem_limit_bytes=24 * 2**20),
        cost_estimate=no_cost,
    )(places, matrix)


def on_device(attention_output, frozen_weight, adapter_down, adapter_up, magnitude, cotangent):
    tensor_count = lax.axis_size("tensor")
    tensor_index = lax.axis_index("tensor")
    fsdp_count = lax.axis_size("fsdp")
    fsdp_index = lax.axis_index("fsdp")
    depth = fsdp_count // 4
    x, y, z = fsdp_index % 2, (fsdp_index // 2) % 2, fsdp_index // 4
    tok_rows, in_rows = attention_output.shape
    rank, output_columns = adapter_up.shape
    own_columns = frozen_weight.shape[1]
    block_columns = output_columns // tensor_count
    plane_columns = output_columns // depth
    block_planes = depth // tensor_count
    grad_scale = (tok_rows * fsdp_count) ** (-0.5)
    across_x = [(i, i ^ 1) for i in range(fsdp_count)]
    across_y = [(i, i ^ 2) for i in range(fsdp_count)]
    z_bits = [1 << i for i in range(2, fsdp_count.bit_length() - 1)]
    planes = chosen_by(
        z, [jnp.array(source_plane(i, depth), jnp.int32)[:, None] for i in range(depth)]
    )
    slots = jnp.arange(4, dtype=jnp.int32)
    owner_of = (4 * planes + 2 * (y ^ (slots // 2)) + (x ^ (slots % 2))).reshape(-1)
    positions = chosen_by(
        z,
        [
            jnp.array([source_plane(i, depth).index(p) for p in range(depth)], jnp.int32)[:, None]
            for i in range(depth)
        ],
    )
    slot_of = (4 * positions + 2 * (y ^ (slots // 2)) + (x ^ (slots % 2))).reshape(-1)
    own_owners = fsdp_count // tensor_count
    own_slots = chosen_by(
        tensor_index, [slot_of[i * own_owners : (i + 1) * own_owners] for i in range(tensor_count)]
    )
    block_offset = tensor_index * block_columns

    def own_block(vector):
        return lax.dynamic_slice_in_dim(vector, block_offset, block_columns, vector.ndim - 1)

    up_own = lax.dynamic_slice_in_dim(adapter_up, fsdp_index * own_columns, own_columns, 1)
    merged = frozen_weight.astype(jnp.float32) + nn(adapter_down, up_own)
    square_own = sum_over(jnp.sum(merged * merged, axis=0), "tensor")

    adapter_hidden = sum_over(nn(attention_output, adapter_down), "tensor").astype(jnp.bfloat16)
    cot_slots = reordered(
        lax.all_gather(cotangent, "tensor", axis=1, tiled=True), owner_of, own_columns
    )
    up_slots = reordered(adapter_up, owner_of, own_columns)
    gram = sum_over(tn(adapter_down, adapter_down), "tensor")

    half = in_rows // 2
    here = jnp.zeros((), jnp.int32)
    all_lanes = slice(None)
    lanes = {"c": slice(0, half), "d": slice(half, in_rows)}
    down_t = adapter_down.T

    def side(bit):
        return (fsdp_index // bit) % 2 == 0

    def widen(value, bit, *token):
        other = flip(tied(value, *token), "fsdp", bit)
        return jnp.concatenate(
            [jnp.where(side(bit), value, other), jnp.where(side(bit), other, value)], axis=-1
        )

    def halve(value, bit, *token):
        middle = value.shape[-1] // 2
        low, high = value[..., :middle], value[..., middle:]
        mine = tied(jnp.where(side(bit), high, low).astype(jnp.bfloat16), *token)
        moved = flip(mine, "fsdp", bit)
        return jnp.where(side(bit), low, high) + moved.astype(jnp.float32)

    def add(value, bit, *token):
        value = tied(value.astype(jnp.bfloat16), *token)
        return (value.astype(jnp.float32) + flip(value, "fsdp", bit).astype(jnp.float32)).astype(
            jnp.bfloat16
        )

    quarter = half // 2
    held = {("whole", way, 0): frozen_weight.T for way in ("own", "up", "down")}

    def send_z(name, hops, *before):
        held[name, "up", hops] = lax.ppermute(
            tied(held[name, "up", hops - 1], *before),
            "fsdp",
            [(i, i + 4) for i in range(fsdp_count - 4) if i // 4 >= hops - 1],
        )
        held[name, "down", hops] = lax.ppermute(
            tied(held[name, "down", hops - 1], *before),
            "fsdp",
            [(i, i - 4) for i in range(4, fsdp_count) if i // 4 + hops - 1 < depth],
        )
        return held[name, "up", hops], held[name, "down", hops]

    def by_z(position, wanted):
        sources = [arrivals(plane, depth)[position] for plane in range(depth)]
        arrays, keys, cases = [], [], []
        for source in sources:
            copies = []
            for name, part, place in wanted:
                key = (name, *source)
                if name in lanes and source[1] <= 1:
                    key = ("whole", *source)
                    part = (all_lanes, lanes[name])
                if key not in keys:
                    keys.append(key)
                    arrays.append(held[key])
                copies.append((keys.index(key), part, place))
            cases.append(copies)
        return cases, arrays

    def own_block_at(position):
        wanted = [(name, all_lanes, (all_lanes, lanes[name])) for name in "cd"]
        if not position:
            return held["whole", "own", 0]
        cases, arrays = by_z(position, wanted)
        return assemble(z, cases, arrays, (own_columns, in_rows))

    finished = []
    running = None

    def across_cores(mine):
        return [mine] + [
            lax.ppermute(
                mine, "tensor", [(i, (i + shift) % tensor_count) for i in range(tensor_count)]
            )
            for shift in range(1, tensor_count)
        ]

    class Columns:
        def __init__(self, cases, sources, slots):
            self.slots = slots
            shape = (len(slots) * own_columns, in_rows)
            self.weight = assemble(z, cases, sources, shape)
            finished.append(self)

        def of(self, matrix):
            parts = [matrix[:, slot * own_columns : (slot + 1) * own_columns] for slot in self.slots]
            return jnp.concatenate(parts, axis=1)

        def forward(self, *token):
            weight = tied(self.weight, *token)
            product = nt(attention_output, weight).astype(jnp.bfloat16)
            self.exchanged = across_cores(product)
            self.cross = nt(down_t, weight)
            return (*self.exchanged, self.cross)

        def complete(self):
            made = complete_columns(
                self.exchanged,
                adapter_hidden,
                self.of(up_slots),
                self.of(cot_slots),
                self.of(scale_slots),
                0,
                own_columns,
            )
            self.layer, self.weighted = made
            return tuple(made)

        def backward(self, *token):
            nonlocal running
            weight = tied(self.weight, *token)
            running = tied(running + nn(self.of(gradient_slots), weight))
            return (running,)

    def rows_of(number):
        return slice(number * own_columns, (number + 1) * own_columns)

    def near(position):
        sources = [own[position], over_x[position], over_y[position]]
        copies = [(i, all_lanes, (rows_of(i), all_lanes)) for i in range(3)]
        return Columns([copies] * depth, sources, [4 * position + i for i in range(3)])

    def far(which):
        cases, sources, slots = [[] for _ in range(depth)], [], []
        for number, position in enumerate(which):
            rows = rows_of(number)
            slots.append(4 * position + 3)
            if position:
                wanted = []
                for i, name in enumerate("cd"):
                    low = lanes[name].start
                    part = (all_lanes, slice(i * quarter, (i + 1) * quarter))
                    wanted.append(("far", part, (rows, slice(low, low + quarter))))
                more, arrays = by_z(position, wanted)
                for case, copies in zip(cases, more):
                    case += [(len(sources) + i, part, place) for i, part, place in copies]
                sources += arrays
            for name, (got, index) in zip("cd", ends[position]):
                low, high = lanes[name].start, lanes[name].stop
                place = (rows, slice(low + quarter if position else low, high))
                for case in cases:
                    case.append((len(sources), rows_of(index), place))
                sources.append(got)
        return Columns(cases, sources, slots)

    def far_halves(which):
        made = []
        for name, came in (("d", over_y), ("c", over_x)):
            low, high = lanes[name].start, lanes[name].stop
            if which != [0]:
                low += quarter
            made.append(jnp.concatenate([came[position][:, low:high] for position in which]))
        return made

    def start_far(which, halves, *before):
        got_d = lax.ppermute(tied(halves[0], *before), "fsdp", across_x)
        got_c = lax.ppermute(tied(halves[1], *before), "fsdp", across_y)
        for number, position in enumerate(which):
            ends[position] = ((got_c, number), (got_d, number))
        return got_c, got_d

    turns = [([0], [], 1), ([], [0], 1)]
    turns += [([position], [], 2) for position in range(1, depth - 1)]
    turns += [([depth - 1], list(range(1, depth - 1)), 3 * depth), ([], [depth - 1], 0)]
    along_z = [("whole", 1)] + [(name, hops) for hops in range(2, depth) for name in "cd"]
    along_z += [("far", hops) for hops in range(1, depth)]
    norms_turn = 2
    summed = False
    sums_turn = depth
    own, over_x, over_y, ends = {}, {}, {}, {}
    squares = square_own
    token = work = ()
    arrived = []
    waiting = []
    for number, (near_planes, far_planes, count_z) in enumerate(turns):
        before = (token, work)
        token = ()
        work = ()
        for position in near_planes:
            own[position] = block = tied(own_block_at(position), *before)
            over_x[position] = lax.ppermute(block, "fsdp", across_x)
            over_y[position] = lax.ppermute(block, "fsdp", across_y)
            token += (over_x[position], over_y[position])
        if far_planes:
            halves = far_halves(far_planes)
            first = token
            token += start_far(far_planes, halves, *before, first)
        if number == norms_turn:
            for bit in z_bits:
                squares = widen(squares, bit, *before)
        sent_z = squares if number == norms_turn else ()
        for name, hops in along_z[:count_z]:
            if name in lanes and hops == 2:
                for way in ("up", "down"):
                    held[name, way, 1] = held["whole", way, 1][:, lanes[name]]
            if name == "far" and hops == 1:
                (got_c, _), (got_d, _) = ends[0]
                block = jnp.concatenate([got_c[:, :quarter], got_d[:, :quarter]], axis=1)
                for way in ("own", "up", "down"):
                    held["far", way, 0] = block
            sent_z = send_z(name, hops, *before, sent_z)
            token += sent_z
            if number == sums_turn and not summed:
                for bit in z_bits:
                    sums = halve(sums, bit, before, sent_z)
                summed = True
                sent_z = (sums,)
        along_z = along_z[count_z:]

        if number < 2:
            squares = widen(squares, (1, 2)[number], *before)
            work += (squares,)
        if number == norms_turn:
            col_norms = jnp.sqrt(squares + eps_norm)
            col_scale = magnitude / col_norms
            scale_slots = reordered(col_scale[None, :], owner_of, own_columns)
            gradient_slots = (cot_slots.astype(jnp.float32) * scale_slots).astype(jnp.bfloat16)
            lowrank_gradient = nt(gradient_slots, up_slots).astype(jnp.bfloat16)
            scale_block = own_block(col_scale)
            grad_block = (cotangent.astype(jnp.float32) * scale_block[None, :]).astype(jnp.bfloat16)
            sums = jnp.concatenate(
                [tn(lowrank_gradient, attention_output), tn(adapter_hidden, grad_block)], axis=1
            )
            running = nn(lowrank_gradient, down_t)
            work += (sums, running)
        if number == sums_turn:
            sums = add(sums, 1)
            work += (sums,)
        if number == sums_turn + 1:
            sums = add(sums, 2, before)

        for columns in arrived:
            work += columns.forward(before)
            waiting.append(columns)
        arrived = [near(position) for position in near_planes]
        if number == sums_turn:
            last_near = arrived.pop()
            work += last_near.forward()
        if far_planes:
            arrived.append(far(far_planes))
        if number == sums_turn:
            for columns in waiting:
                work += columns.complete()
                if len(columns.slots) == 3:
                    work += columns.backward(before)
            done = waiting
            waiting = [last_near]
    for bit in reversed(z_bits):
        sums = widen(sums, bit)
    in_sum = sums[:, :in_rows].astype(jnp.float32)
    up_sum = sums[:, in_rows:].astype(jnp.float32)

    for columns in arrived:
        columns.forward(token)
        waiting.append(columns)
    for columns in waiting:
        columns.complete()
    waiting = [columns for columns in done if len(columns.slots) != 3] + waiting
    input_gradient = last_gradient(
        [columns.of(gradient_slots) for columns in waiting],
        [columns.weight for columns in waiting],
        running,
    )
    order = [slot for columns in finished for slot in columns.slots]
    place = jnp.array([order.index(slot) for slot in range(fsdp_count)], jnp.int32)

    def joined_columns(parts, places):
        return reordered(jnp.concatenate(parts, axis=1), place[places], own_columns)

    layer_out = joined_columns([columns.layer for columns in finished], own_slots)

    weighted_parts = [columns.weighted for columns in finished]
    weighted_sum = sum_over(joined_columns(weighted_parts, slot_of)[0], "fsdp")
    weighted = weighted_sum / col_norms
    coef = -weighted * magnitude / (col_norms * col_norms)
    scaled_up = (adapter_up.astype(jnp.float32) * coef[None, :]).astype(jnp.bfloat16)
    up_inner = nt(scaled_up, adapter_up)
    scaled_slots = reordered(scaled_up, owner_of, own_columns)
    norm_down = sum(nn(part.of(scaled_slots), part.weight) for part in finished)
    inner_down = lax.dot_general(
        up_inner,
        adapter_down.astype(jnp.float32),
        (((1,), (1,)), ((), ())),
        precision=lax.Precision.HIGHEST,
    )
    down_gradient = ((in_sum + norm_down + inner_down) * grad_scale).T
    crossed = across_cores(jnp.concatenate([columns.cross for columns in finished], axis=1))
    project = joined_columns([sum(crossed[1:], crossed[0])], own_slots) + jnp.dot(
        gram, own_block(adapter_up).astype(jnp.float32), precision=lax.Precision.HIGHEST
    )
    d_up = (up_sum + project * own_block(coef)[None, :]) * grad_scale
    d_magnitude = own_block(weighted) * grad_scale
    return (layer_out, input_gradient, down_gradient, d_up, d_magnitude)


def solution(mesh):
    return jax.shard_map(
        on_device,
        mesh=mesh,
        in_specs=(
            P("fsdp", "tensor"),
            P("tensor", "fsdp"),
            P("tensor", None),
            P(),
            P(),
            P("fsdp", "tensor"),
        ),
        out_specs=(
            P("fsdp", "tensor"),
            P("fsdp", "tensor"),
            P("tensor", None),
            P(None, "tensor"),
            P("tensor"),
        ),
        check_vma=False,
    )
```
